256 devices in a mesh: crop: 2 (over core), row: 8 (over z), col: 16 (over y, x).
Axes of the slice: x: 4, y: 4, z: 8, core: 2. Of those that a mesh axis runs over, the one named last changes fastest.
Arguments:
- pair: float32 [2, 512, 512, 128], P('crop', 'row', 'col'), parts along dimension 0, may hold values from -6 to 6
- gain_input: float32 [128], replicated, may hold values from 0.1 to 1.9
- weights_in: float32 [128, 512], replicated, may hold values from -0.5 to 0.5
- gate_weights: float32 [128, 128], replicated, may hold values from -0.5 to 0.5
- weights_out: float32 [128, 128], replicated, may hold values from -0.5 to 0.5
- gain_product: float32 [128], replicated, may hold values from 0.1 to 1.9
- gain_transition: float32 [128], replicated, may hold values from 0.1 to 1.9
- transition_in: float32 [128, 1024], replicated, may hold values from -0.5 to 0.5
- transition_out: float32 [512, 128], replicated, may hold values from -0.25 to 0.25
- distogram_weights: float32 [128, 64], replicated, may hold values from -0.5 to 0.5
- distogram_bias: float32 [64], replicated, may hold values from -4 to 4
Outputs:
- logits: float32 [2, 512, 512, 64], P('crop', 'row', 'col'), parts along dimension 0
The draws below stay inside these ranges and needn't reach their ends.
There are 2 independent parts, one for each index of `crop`. The reference program is written for one: setup_inputs(seed, part) draws one part's arguments, and reference() takes and returns one part's arrays. A program takes and returns all parts, laid end to end along the dimension named above; an argument that names none is the same for every part. Nothing has to cross between parts.
All inputs are finite; a program needn't handle non-finite values.
Results may differ from the reference program's by a relative error of at most 0.00007.
Values sent between devices are 32-bit elements; how exact they have to be, the bound alone decides.
A program may use at most 64 MiB of HBM per device.

```python
import jax
import jax.numpy as jnp
from jax import lax

PAIR_W = 128
HIDDEN_SIZE = 512
BINS = 64
TOKENS = 512
CROPS = 1


def block_scale(key, shape, cuts, least, top_value):
    factor_of, own = 1.0, jax.random.fold_in(key, 6)
    for dim, shards_of in cuts:
        heights = jnp.exp(jax.random.uniform(jax.random.fold_in(own, dim), (shards_of,), jnp.float32, least / len(cuts), top_value / len(cuts)))
        factor_of = factor_of * jnp.repeat(heights, shape[dim] // shards_of).reshape([-1 if axis == dim else 1 for axis in range(len(shape))])
    return factor_of


def bell_draw(own_key, dims, scale, reach, split=(), held_as=jnp.bfloat16):
    factor_of = block_scale(own_key, dims, split, -0.22, 0.18) if split else 1.0
    result = jax.random.normal(own_key, dims, jnp.float32) * scale * factor_of
    return jnp.minimum(jnp.maximum(result, -reach), reach).astype(held_as)


def setup_inputs(seed: int = 0, part: int = 0) -> dict:
    key_of = jax.random.split(jax.random.key(seed), 12)
    part_splits = jax.random.split(jax.random.fold_in(key_of[11], part), 12)
    return {
        "pair": bell_draw(part_splits[0], (CROPS, TOKENS, TOKENS, PAIR_W), 1.0, 6.0, ((1, 8), (2, 16)), jnp.float32),
        "gain_input": jnp.clip(1.0 + 0.18 * jax.random.normal(key_of[1], (PAIR_W,), jnp.float32), 0.1, 1.9),
        "weights_in": bell_draw(key_of[2], (PAIR_W, 4 * PAIR_W), PAIR_W ** -0.5, 0.5, (), jnp.float32),
        "gate_weights": bell_draw(key_of[3], (PAIR_W, PAIR_W), PAIR_W ** -0.5, 0.5, (), jnp.float32),
        "weights_out": bell_draw(key_of[4], (PAIR_W, PAIR_W), PAIR_W ** -0.5, 0.5, (), jnp.float32),
        "gain_product": jnp.clip(1.0 + 0.18 * jax.random.normal(key_of[5], (PAIR_W,), jnp.float32), 0.1, 1.9),
        "gain_transition": jnp.clip(1.0 + 0.18 * jax.random.normal(key_of[6], (PAIR_W,), jnp.float32), 0.1, 1.9),
        "transition_in": bell_draw(key_of[7], (PAIR_W, 2 * HIDDEN_SIZE), PAIR_W ** -0.5, 0.5, (), jnp.float32),
        "transition_out": bell_draw(key_of[8], (HIDDEN_SIZE, PAIR_W), HIDDEN_SIZE ** -0.5, 0.25, (), jnp.float32),
        "distogram_weights": bell_draw(key_of[9], (PAIR_W, BINS), PAIR_W ** -0.5, 0.5, (), jnp.float32),
        "distogram_bias": bell_draw(key_of[10], (BINS,), 1.0, 4.0, (), jnp.float32),
    }


HIGH = lax.Precision.HIGHEST

def layer_norm(values, gain):
    center = values - lax.optimization_barrier(jnp.mean(values, axis=-1, keepdims=True))
    spread = lax.optimization_barrier(jnp.mean(center * center, axis=-1, keepdims=True))
    return center * lax.rsqrt(spread + 1e-05) * gain

def project(values, weights):
    return jnp.einsum('...c,cd->...d', values, weights, precision=HIGH)

def reference(pair, gain_input, weights_in, gate_weights, weights_out, gain_product, gain_transition, transition_in, transition_out, distogram_weights, distogram_bias):

    def one_crop(square):
        normed = layer_norm(square, gain_input)
        projected = project(normed, weights_in)
        left_hand = jax.nn.sigmoid(projected[..., PAIR_W:2 * PAIR_W]) * projected[..., :PAIR_W]
        right_hand = jax.nn.sigmoid(projected[..., 3 * PAIR_W:]) * projected[..., 2 * PAIR_W:3 * PAIR_W]
        product = jnp.einsum('ikc,jkc->ijc', left_hand, right_hand, precision=HIGH)
        gate = jax.nn.sigmoid(project(normed, gate_weights))
        updated = square + gate * project(layer_norm(product, gain_product), weights_out)

        def transition(line):
            hidden = project(layer_norm(line, gain_transition), transition_in)
            activated = jax.nn.silu(hidden[:, :HIDDEN_SIZE]) * hidden[:, HIDDEN_SIZE:]
            return line + project(activated, transition_out)
        pair_out = lax.map(transition, updated)
        symmetric = pair_out + jnp.swapaxes(pair_out, 0, 1)
        return project(symmetric, distogram_weights) + distogram_bias
    return lax.map(one_crop, pair)
```

```python
import functools

import jax
import jax.numpy as jnp
from jax import lax
from jax.experimental import pallas as pl
from jax.experimental.pallas import tpu as pltpu
from jax.sharding import PartitionSpec as P

MESH = pl.DeviceIdType.MESH
BF = jnp.bfloat16
F32 = jnp.float32
NZ = 8
NQ = 16

LR_XY, LR_Z, BASE, P_Z, P_XY, A1_XY, A2_Z, A2_XY, PHASES = 0, 4, 8, 9, 11, 13, 15, 17, 19


def split(values):
    high = values.astype(BF)
    return high, (values - high.astype(F32)).astype(BF)


def stack_right(values):
    high, low = split(values)
    return jnp.concatenate([high, low, high], axis=0)


def normalize(values):
    center = values - jnp.mean(values, axis=0, keepdims=True)
    spread = jnp.mean(center * center, axis=0, keepdims=True)
    return center * lax.rsqrt(spread + 1e-05)


def dot(left, right):
    return lax.dot_general(left, right, (((1,), (0,)), ((), ())), preferred_element_type=F32)


def dot_nt(left, right):
    return lax.dot_general(left, right, (((1,), (1,)), ((), ())), preferred_element_type=F32)


def sigmoid(values):
    return 1.0 / (1.0 + jnp.exp(-values))


def store_weights(target, row, weights, gain):
    depth = weights.shape[0]
    for part in range(depth // 128):
        turned = weights[part * 128 : (part + 1) * 128, :].T
        if gain is not None:
            turned = turned * gain
        high, low = split(turned)
        rows = pl.ds(row, turned.shape[0])
        at = part * 128
        target[rows, at : at + 128] = high
        target[rows, depth + at : depth + at + 128] = high
        target[rows, 2 * depth + at : 2 * depth + at + 128] = low


def kernel(
    pair,
    gain_in,
    w_in,
    w_gate,
    w_out,
    gain_prod,
    gain_trans,
    w_ti,
    w_to,
    w_dist,
    bias,
    out,
    win3,
    wgate3,
    wout3,
    wti3,
    wto3,
    wdist3,
    x3,
    sb1,
    rb1,
    sb2,
    rb2,
    base,
    xt,
    gate,
    r3,
    psb,
    prb,
    psx,
    prx,
    abuf,
    a1,
    a2m,
    a2f,
    send_sem,
    recv_sem,
):
    crop = lax.axis_index("crop")
    z = lax.axis_index("row")
    q = lax.axis_index("col")

    def to_plane(phase, source, target, count=NQ):
        def step(k, carry):
            peer = lax.rem(q + k, NQ)
            pltpu.make_async_remote_copy(
                src_ref=source(peer),
                dst_ref=target,
                send_sem=send_sem.at[phase],
                recv_sem=recv_sem.at[phase],
                device_id=(crop, z, peer),
                device_id_type=MESH,
            ).start()
            return carry

        lax.fori_loop(1, NQ, step, 0)
        pltpu.make_async_copy(source(q), target, recv_sem.at[phase]).start()

    def to_line(phase, source, target):
        def step(k, carry):
            peer = lax.rem(z + k, NZ)
            pltpu.make_async_remote_copy(
                src_ref=source(peer),
                dst_ref=target,
                send_sem=send_sem.at[phase],
                recv_sem=recv_sem.at[phase],
                device_id=(crop, peer, q),
                device_id_type=MESH,
            ).start()
            return carry

        lax.fori_loop(1, NZ, step, 0)
        pltpu.make_async_copy(source(z), target, recv_sem.at[phase]).start()

    def landed(phase, whole):
        pltpu.make_async_copy(whole, whole, recv_sem.at[phase]).wait()

    def sent(phase, most):
        pltpu.make_async_copy(most, most, send_sem.at[phase]).wait()

    barrier = pltpu.get_barrier_semaphore()

    def greet_plane(k, carry):
        pl.semaphore_signal(barrier, inc=1, device_id=(crop, z, lax.rem(q + k, NQ)), device_id_type=MESH)
        return carry

    def greet_line(k, carry):
        pl.semaphore_signal(barrier, inc=1, device_id=(crop, lax.rem(z + k, NZ), q), device_id_type=MESH)
        return carry

    lax.fori_loop(1, NQ, greet_plane, 0)
    lax.fori_loop(1, NZ, greet_line, 0)

    for block in range(4):
        store_weights(win3, block * 128, w_in[:, block * 128 : (block + 1) * 128], gain_in[...])

    def norm_chunk(h):
        def step(n, carry):
            blocks = []
            for u in range(4):
                rows = pair[:, h * 2 : h * 2 + 2, n * 4 + u, :, :]
                blocks.append(rows.reshape(128, 128).T)
            x3[h * 2 + n] = stack_right(normalize(jnp.concatenate(blocks, axis=1)))
            return carry

        lax.fori_loop(0, 2, step, 0)

    def project_chunk(side, h):
        first = 256 if side == 0 else 0

        def step(n, carry):
            both = dot(win3[first : first + 256, :], x3[h * 2 + n])
            value = sigmoid(both[128:, :]) * both[:128, :]
            for u in range(4):
                at = pl.multiple_of((n * 4 + u) * 8, 8)
                sb1[side * 2 + h, :, pl.ds(at, 8), :] = value[:, u * 128 : (u + 1) * 128].reshape(16, 8, 128)
            return carry

        lax.fori_loop(0, 2, step, 0)
        index = side * 2 + h
        to_plane(LR_XY + index, lambda peer: sb1.at[index, peer], rb1.at[index, q])

    lane = lax.broadcasted_iota(jnp.int32, (8, 128), 1)
    low_half = lane < 64
    even_block = lax.rem(lane, 64) < 32

    def relay_chunk(index):
        landed(LR_XY + index, rb1.at[index])

        def step(c, carry):
            for group in range(4):
                v = [rb1[index, group * 4 + u, pl.ds(c, 8, stride=8), :] for u in range(4)]
                s = [None] * 4
                for u in range(2):
                    s[u] = jnp.where(low_half, v[u], pltpu.roll(v[u + 2], 64, 1))
                    s[u + 2] = jnp.where(low_half, pltpu.roll(v[u], 64, 1), v[u + 2])
                for u in (0, 2):
                    first = jnp.where(even_block, s[u], pltpu.roll(s[u + 1], 32, 1))
                    second = jnp.where(even_block, pltpu.roll(s[u], 96, 1), s[u + 1])
                    lanes = slice(group * 128, (group + 1) * 128)
                    sb2[index, c, u * 8 : u * 8 + 8, lanes] = first
                    sb2[index, c, u * 8 + 8 : u * 8 + 16, lanes] = second
            return carry

        lax.fori_loop(0, 8, step, 0)
        to_line(LR_Z + index, lambda peer: sb2.at[index, peer], rb2.at[index, z])

    norm_chunk(0)
    project_chunk_ready = pl.semaphore_wait(barrier, NQ - 1 + NZ - 1)
    del project_chunk_ready
    project_chunk(0, 0)
    norm_chunk(1)
    project_chunk(0, 1)
    project_chunk(1, 0)
    relay_chunk(0)
    project_chunk(1, 1)
    relay_chunk(1)

    def pair_source(peer):
        return pair.at[peer // 8, :, lax.rem(peer, 8)]

    to_plane(BASE, pair_source, base.at[q])
    relay_chunk(2)
    relay_chunk(3)

    store_weights(wgate3, 0, w_gate[...], gain_in[...])
    store_weights(wout3, 0, w_out[...], gain_prod[...])
    for block in range(8):
        store_weights(wti3, block * 128, w_ti[:, block * 128 : (block + 1) * 128], gain_trans[...])
    store_weights(wto3, 0, w_to[...], None)
    store_weights(wdist3, 0, w_dist[...], None)

    landed(BASE, base)

    def base_step(hb, carry):
        blocks = [base[g * 4 : g * 4 + 4, hb].reshape(128, 128).T for g in range(4)]
        value = jnp.concatenate(blocks, axis=1)
        xt[hb] = value
        gate[hb] = sigmoid(dot(wgate3[...], stack_right(normalize(value))))
        return carry

    lax.fori_loop(0, 4, base_step, 0)

    for h in range(2):
        landed(LR_Z + h, rb2.at[h])

        def right_step(n, carry):
            zz, a = n // 2, lax.rem(n, 2)
            high, low = split(rb2[h, zz, pl.ds(pl.multiple_of(a * 16, 16), 16), :])
            rows = pl.ds(pl.multiple_of(zz * 64 + a * 32 + h * 16, 16), 16)
            r3[rows, 0:512] = high
            r3[rows, 512:1024] = low
            r3[rows, 1024:1536] = high
            return carry

        lax.fori_loop(0, 16, right_step, 0)

    for h in range(2):
        landed(LR_Z + 2 + h, rb2.at[2 + h])
        high, low = split(rb2[2 + h].reshape(256, 512))
        l3 = jnp.concatenate([high, high, low], axis=1)
        for jt in range(4):
            product = dot_nt(l3, r3[jt * 128 : (jt + 1) * 128, :])
            for zz in range(8):
                at = zz * 128 + jt * 32
                psb[h, at : at + 32, :] = product[zz * 32 : (zz + 1) * 32, :]
        to_line(
            P_Z + h,
            lambda peer: psb.at[h, pl.ds(pl.multiple_of(peer * 128, 128), 128), :],
            prb.at[h, pl.ds(pl.multiple_of(z * 128, 128), 128), :],
        )

    def product_relay(h):
        landed(P_Z + h, prb.at[h])

        def step(row, carry):
            m = (row // 16) * 8 + lax.rem(row, 8)
            b = lax.rem(row // 8, 2)
            for jt in range(4):
                psx[h, m, b * 4 + jt] = prb[h, pl.ds(jt * 32 + row, 8, stride=128), :]
            return carry

        lax.fori_loop(0, 32, step, 0)
        to_plane(P_XY + h, lambda peer: psx.at[h, peer], prx.at[h, q])

    def transition(h):
        landed(P_XY + h, prx.at[h])
        logits = []
        for b in range(2):
            hb = h * 2 + b
            product = jnp.concatenate([prx[h, :, b * 4 + jt].reshape(128, 128) for jt in range(4)], axis=1)
            updated = xt[hb] + gate[hb] * dot(wout3[...], stack_right(normalize(product)))
            right = stack_right(normalize(updated))
            total = updated
            for part in range(2):
                at = part * 256
                up_gate = dot(wti3[at : at + 256, :], right)
                up = dot(wti3[512 + at : 768 + at, :], right)
                high, low = split(up_gate * sigmoid(up_gate) * up)
                total = total + dot(wto3[:, at : at + 256], high)
                total = total + dot(wto3[:, 512 + at : 768 + at], low)
                total = total + dot(wto3[:, 1024 + at : 1280 + at], high)
            logits.append(dot(wdist3[...], stack_right(total)))
        stacked = jnp.concatenate(logits, axis=0)
        for jt in range(4):
            abuf[h, jt * 128 : (jt + 1) * 128, :] = stacked[:, jt * 128 : (jt + 1) * 128].T
        to_line(
            A2_Z + h,
            lambda peer: abuf.at[h, pl.ds(pl.multiple_of(peer * 64, 64), 64), :],
            a2m.at[h, z],
        )
        to_plane(
            A1_XY + h,
            lambda peer: abuf.at[h, pl.ds(pl.multiple_of(peer * 32, 32), 32), :],
            a1.at[h, q],
        )

    own = lax.rem(q, 2) == q // 8

    def mirror_relay(h):
        landed(A2_Z + h, a2m.at[h])
        target = a2f.at[h, pl.ds(pl.multiple_of(lax.rem(q, 8) * 64, 64), 64), :]

        def step(k, carry):
            zz = lax.rem(z + k, NZ)
            peer = 2 * zz + q // 8

            @pl.when(peer != q)
            def _():
                pltpu.make_async_remote_copy(
                    src_ref=a2m.at[h, zz],
                    dst_ref=target,
                    send_sem=send_sem.at[A2_XY + h],
                    recv_sem=recv_sem.at[A2_XY + h],
                    device_id=(crop, z, peer),
                    device_id_type=MESH,
                ).start()

            @pl.when(peer == q)
            def _():
                pltpu.make_async_copy(a2m.at[h, zz], target, recv_sem.at[A2_XY + h]).start()

            return carry

        lax.fori_loop(0, NZ, step, 0)

    product_relay(0)
    transition(0)
    product_relay(1)
    mirror_relay(0)
    transition(1)
    mirror_relay(1)

    for h in range(2):
        landed(A1_XY + h, a1.at[h])
        landed(A2_XY + h, a2f.at[h])

    both_bias = jnp.concatenate([bias[...], bias[...]], axis=1)

    def final_step(m, carry):
        first = (m // 8) * 32 + lax.rem(m, 8)
        for h in range(2):
            for h2 in range(2):
                mine = [a1[h, m, h2 * 16 + b2 * 8 : h2 * 16 + b2 * 8 + 8, :] + both_bias for b2 in range(2)]
                for b in range(2):
                    i = first + h * 16 + b * 8
                    other = a2f[h2, pl.ds(i, 8, stride=64), :]
                    turned = pltpu.roll(other, 64, 1)
                    for b2 in range(2):
                        value = mine[b2] + (other if b == b2 else turned)
                        if b:
                            value = pltpu.roll(value, 64, 1)
                        out[i, h2 * 16 + b2 * 8 : h2 * 16 + b2 * 8 + 8, :] = value[:, :64]
        return carry

    lax.fori_loop(0, NQ, final_step, 0)

    for index in range(4):
        sent(LR_XY + index, sb1.at[index, pl.ds(0, NQ - 1)])
        sent(LR_Z + index, sb2.at[index, pl.ds(0, NZ - 1)])
    sent(BASE, base.at[pl.ds(0, NQ - 1)])
    for h in range(2):
        sent(P_Z + h, psb.at[h, pl.ds(0, 128 * (NZ - 1)), :])
        sent(P_XY + h, psx.at[h, pl.ds(0, NQ - 1)])
        sent(A1_XY + h, abuf.at[h, pl.ds(0, 32 * (NQ - 1)), :])
        sent(A2_Z + h, abuf.at[h, pl.ds(0, 64 * (NZ - 1)), :])

        @pl.when(own)
        def _():
            sent(A2_XY + h, a2m.at[h, pl.ds(0, NZ - 1)])

        @pl.when(jnp.logical_not(own))
        def _():
            sent(A2_XY + h, a2m.at[h])


def shards(pair, gain_in, w_in, w_gate, w_out, gain_prod, gain_trans, w_ti, w_to, w_dist, bias):
    vmem = pl.BlockSpec(memory_space=pltpu.VMEM)
    result = pl.pallas_call(
        kernel,
        out_shape=jax.ShapeDtypeStruct((64, 32, 64), F32),
        in_specs=[vmem] * 11,
        out_specs=vmem,
        scratch_shapes=[
            pltpu.VMEM((512, 384), BF),
            pltpu.VMEM((128, 384), BF),
            pltpu.VMEM((128, 384), BF),
            pltpu.VMEM((1024, 384), BF),
            pltpu.VMEM((128, 1536), BF),
            pltpu.VMEM((64, 384), BF),
            pltpu.VMEM((4, 384, 512), BF),
            pltpu.VMEM((4, 16, 64, 128), F32),
            pltpu.VMEM((4, 16, 64, 128), F32),
            pltpu.VMEM((4, 8, 32, 512), F32),
            pltpu.VMEM((4, 8, 32, 512), F32),
            pltpu.VMEM((16, 4, 32, 128), F32),
            pltpu.VMEM((4, 128, 512), F32),
            pltpu.VMEM((4, 128, 512), F32),
            pltpu.VMEM((512, 1536), BF),
            pltpu.VMEM((2, 1024, 128), F32),
            pltpu.VMEM((2, 1024, 128), F32),
            pltpu.VMEM((2, 16, 8, 8, 128), F32),
            pltpu.VMEM((2, 16, 8, 8, 128), F32),
            pltpu.VMEM((2, 512, 128), F32),
            pltpu.VMEM((2, 16, 32, 128), F32),
            pltpu.VMEM((2, 8, 64, 128), F32),
            pltpu.VMEM((2, 512, 128), F32),
            pltpu.SemaphoreType.DMA((PHASES,)),
            pltpu.SemaphoreType.DMA((PHASES,)),
        ],
        compiler_params=pltpu.CompilerParams(
            collective_id=0, has_side_effects=True, vmem_limit_bytes=56 * 1024 * 1024
        ),
        name="triangle",
    )(
        pair.reshape(2, 4, 8, 32, 128),
        gain_in.reshape(1, 128),
        w_in,
        w_gate,
        w_out,
        gain_prod.reshape(1, 128),
        gain_trans.reshape(1, 128),
        w_ti,
        w_to,
        w_dist,
        bias.reshape(1, 64),
    )
    return result.reshape(1, 64, 32, 64)


def solution(mesh):
    return jax.shard_map(
        shards,
        mesh=mesh,
        in_specs=(P("crop", "row", "col", None), P(), P(), P(), P(), P(), P(), P(), P(), P(), P()),
        out_specs=P("crop", "row", "col", None),
        check_vma=False,
    )
```

```python
import jax
import jax.numpy as jnp
from jax import lax
from jax.experimental import pallas as pl
from jax.experimental.pallas import tpu as pltpu
from jax.sharding import PartitionSpec as P

MESH = pl.DeviceIdType.MESH
BF = jnp.bfloat16
F32 = jnp.float32
NZ = 8
NQ = 16
ND = NZ * NQ

LR, BASE, PROD, A1, A2Z, A2Q, PHASES = 0, 4, 5, 7, 11, 15, 19


def split(values):
    high = values.astype(BF)
    return high, (values - high.astype(F32)).astype(BF)


def stack_right(values):
    high, low = split(values)
    return jnp.concatenate([high, low, high], axis=0)


def normalize(values):
    center = values - jnp.mean(values, axis=0, keepdims=True)
    spread = jnp.mean(center * center, axis=0, keepdims=True)
    return center * lax.rsqrt(spread + 1e-05)


def dot(left, right):
    return lax.dot_general(left, right, (((1,), (0,)), ((), ())), preferred_element_type=F32)


def dot_nt(left, right):
    return lax.dot_general(left, right, (((1,), (1,)), ((), ())), preferred_element_type=F32)


def sigmoid(values):
    return 1.0 / (1.0 + jnp.exp(-values))


def store_weights(target, row, weights, gain, turn=True):
    depth = weights.shape[0] if turn else 128
    for part in range(depth // 128):
        turned = weights[part * 128 : (part + 1) * 128, :].T if turn else weights
        if gain is not None:
            turned = turned * gain
        high, low = split(turned)
        rows = pl.ds(row, turned.shape[0])
        at = part * 128
        target[rows, at : at + 128] = high
        target[rows, depth + at : depth + at + 128] = high
        target[rows, 2 * depth + at : 2 * depth + at + 128] = low


def kernel(
    pair,
    gain_in,
    w_in,
    w_gate,
    w_out,
    gain_prod,
    gain_trans,
    w_ti,
    w_to,
    w_dist,
    bias,
    out,
    win3,
    wgate3,
    wout3,
    wti3,
    wto3,
    wdist3,
    x3,
    sb,
    rb,
    base,
    xt,
    gate,
    right_high,
    right_low,
    left_high,
    left_low,
    psb,
    prb,
    abuf,
    a1,
    a2m,
    a2f,
    send_sem,
    recv_sem,
    line_sem,
):
    crop = lax.axis_index("crop")
    z = lax.axis_index("row")
    q = lax.axis_index("col")
    me = z * NQ + q

    def remote(phase, source, target, zz, qq):
        pltpu.make_async_remote_copy(
            src_ref=source,
            dst_ref=target,
            send_sem=send_sem.at[phase],
            recv_sem=recv_sem.at[phase],
            device_id=(crop, zz, qq),
            device_id_type=MESH,
        ).start()

    def local(phase, source, target):
        pltpu.make_async_copy(source, target, recv_sem.at[phase]).start()

    def to_all(phase, source, target, beside=None):
        with jax.named_scope("issue_%d" % phase):
            for k in range(1, NZ):
                zz = lax.rem(z + k, NZ)
                remote(phase, source(zz * NQ + q), target, zz, q)

            def step(k, carry):
                qq = lax.rem(q + k, NQ)
                for kz in range(NZ):
                    zz = lax.rem(z + kz, NZ)
                    remote(phase, source(zz * NQ + qq), target, zz, qq)
                if beside is not None:
                    beside(qq)
                return carry

            lax.fori_loop(1, NQ, step, 0)
            local(phase, source(me), target)

    def to_plane(phase, source, target):
        def step(k, carry):
            qq = lax.rem(q + k, NQ)
            remote(phase, source(qq), target, z, qq)
            return carry

        lax.fori_loop(1, NQ, step, 0)
        local(phase, source(q), target)

    def to_line(phase, source, target):
        for k in range(1, NZ):
            zz = lax.rem(z + k, NZ)
            remote(phase, source(zz), target, zz, q)
        local(phase, source(z), target)

    def landed(phase, whole):
        with jax.named_scope("wait_%d" % phase):
            pltpu.make_async_copy(whole, whole, recv_sem.at[phase]).wait()

    def sent(phase, most):
        pltpu.make_async_copy(most, most, send_sem.at[phase]).wait()

    barrier = pltpu.get_barrier_semaphore()

    def greet_plane(k, carry):
        pl.semaphore_signal(barrier, inc=1, device_id=(crop, z, lax.rem(q + k, NQ)), device_id_type=MESH)
        return carry

    lax.fori_loop(1, NQ, greet_plane, 0)
    for k in range(1, NZ):
        pl.semaphore_signal(barrier, inc=1, device_id=(crop, lax.rem(z + k, NZ), q), device_id_type=MESH)

    for block in (2, 3, 0, 1):
        store_weights(win3, block * 128, w_in[:, block * 128 : (block + 1) * 128], gain_in[...])

    def norm_chunk(h):
        def step(n, carry):
            blocks = []
            for u in range(4):
                rows = pair[:, h * 2 : h * 2 + 2, n * 4 + u, :, :]
                blocks.append(rows.reshape(128, 128).T)
            x3[h * 2 + n] = stack_right(normalize(jnp.concatenate(blocks, axis=1)))
            return carry

        with jax.named_scope("norm"):
            lax.fori_loop(0, 2, step, 0)

    def project_chunk(side, h):
        first = 256 if side == 0 else 0
        index = side * 2 + h

        def step(n, carry):
            both = dot(win3[first : first + 256, :], x3[h * 2 + n])
            value = sigmoid(both[128:, :]) * both[:128, :]
            for u in range(4):
                sb[index, pl.ds(n * 4 + u, 128, stride=8), :] = value[:, u * 128 : (u + 1) * 128]
            return carry

        with jax.named_scope("project"):
            lax.fori_loop(0, 2, step, 0)

    def send_chunk(index, beside=None):
        to_all(
            LR + index,
            lambda p: sb.at[index, pl.ds(pl.multiple_of(p * 8, 8), 8), :],
            rb.at[index, me],
            beside,
        )

    def pair_source(peer):
        return pair.at[peer // 8, :, lax.rem(peer, 8)]

    norm_chunk(0)
    with jax.named_scope("wait_barrier"):
        pl.semaphore_wait(barrier, NQ - 1 + NZ - 1)
    for k in range(1, NZ):
        pl.semaphore_signal(line_sem, inc=1, device_id=(crop, lax.rem(z + k, NZ), q), device_id_type=MESH)
    project_chunk(0, 0)
    with jax.named_scope("wait_line"):
        pl.semaphore_wait(line_sem, NZ - 1)
    send_chunk(0)
    norm_chunk(1)
    project_chunk(0, 1)
    send_chunk(1)
    project_chunk(1, 0)
    send_chunk(2, lambda qq: remote(BASE, pair_source(qq), base.at[q], z, qq))
    local(BASE, pair_source(q), base.at[q])
    project_chunk(1, 1)
    send_chunk(3)

    with jax.named_scope("weights"):
        store_weights(wgate3, 0, w_gate[...], gain_in[...])
        store_weights(wout3, 0, w_out[...], gain_prod[...])
        for block in range(8):
            store_weights(wti3, block * 128, w_ti[:, block * 128 : (block + 1) * 128], gain_trans[...])
        store_weights(wto3, 0, w_to[...], None)
        store_weights(wdist3, 0, w_dist[...], None, turn=False)

    lane = lax.broadcasted_iota(jnp.int32, (8, 128), 1)
    low_half = lane < 64
    even_block = lax.rem(lane, 64) < 32

    def assemble(index, high_ref, low_ref, first):
        landed(LR + index, rb.at[index])

        def step(zz, carry):
            for group in range(4):
                v = [rb[index, zz * NQ + group * 4 + u] for u in range(4)]
                s = [None] * 4
                for u in range(2):
                    s[u] = jnp.where(low_half, v[u], pltpu.roll(v[u + 2], 64, 1))
                    s[u + 2] = jnp.where(low_half, pltpu.roll(v[u], 64, 1), v[u + 2])
                for a in range(2):
                    even, odd = s[2 * a], s[2 * a + 1]
                    both = jnp.concatenate(
                        [
                            jnp.where(even_block, even, pltpu.roll(odd, 32, 1)),
                            jnp.where(even_block, pltpu.roll(even, 96, 1), odd),
                        ],
                        axis=0,
                    )
                    high, low = split(both)
                    rows = pl.ds(pl.multiple_of(first + zz * 32 + a * 16, 16), 16)
                    high_ref[rows, group * 128 : (group + 1) * 128] = high
                    low_ref[rows, group * 128 : (group + 1) * 128] = low
            return carry

        with jax.named_scope("assemble"):
            lax.fori_loop(0, NZ, step, 0)

    assemble(0, right_high, right_low, 0)
    assemble(1, right_high, right_low, 256)

    def multiply(h):
        assemble(2 + h, left_high, left_low, 0)
        with jax.named_scope("product"):
            for half in range(2):
                rows = slice(half * 256, half * 256 + 256)
                product = (
                    dot_nt(left_high[...], right_high[rows, :])
                    + dot_nt(left_high[...], right_low[rows, :])
                    + dot_nt(left_low[...], right_high[rows, :])
                )
                for zz in range(NZ):
                    for a in range(2):
                        for b in range(2):
                            row = zz * 32 + a * 16 + b * 8
                            for u in range(2):
                                start = (zz * 16 + a * 8) * 8 + b * 4 + half * 2 + u
                                psb[h, pl.ds(start, 8, stride=8), :] = product[row : row + 8, u * 128 : (u + 1) * 128]
        to_all(
            PROD + h,
            lambda p: psb.at[h, pl.ds(pl.multiple_of(p * 8, 8), 8), :],
            prb.at[h, pl.ds(pl.multiple_of(me * 8, 8), 8), :],
        )

    multiply(0)
    landed(BASE, base)

    def base_step(hb, carry):
        blocks = []
        for jt in range(4):
            some = base[(jt % 2) * 8 : (jt % 2) * 8 + 8, hb, (jt // 2) * 16 : (jt // 2) * 16 + 16, :]
            blocks.append(some.reshape(128, 128).T)
        value = jnp.concatenate(blocks, axis=1)
        xt[hb] = value
        gate[hb] = sigmoid(dot(wgate3[...], stack_right(normalize(value))))
        return carry

    with jax.named_scope("base_gate"):
        lax.fori_loop(0, 4, base_step, 0)
    multiply(1)

    target = pl.ds(pl.multiple_of(lax.rem(q, 8) * 32, 32), 32)

    def transition(h, b):
        hb = h * 2 + b
        with jax.named_scope("transition"):
            product = jnp.concatenate(
                [prb[h, pl.ds(b * 4 + jt, 128, stride=8), :] for jt in range(4)], axis=1
            )
            updated = xt[hb] + gate[hb] * dot(wout3[...], stack_right(normalize(product)))
            right = stack_right(normalize(updated))
            total = updated
            for part in range(2):
                at = part * 256
                up_gate = dot(wti3[at : at + 256, :], right)
                up = dot(wti3[512 + at : 768 + at, :], right)
                high, low = split(up_gate * sigmoid(up_gate) * up)
                total = total + dot(wto3[:, at : at + 256], high)
                total = total + dot(wto3[:, 512 + at : 768 + at], low)
                total = total + dot(wto3[:, 1024 + at : 1280 + at], high)
            logits = dot(wdist3[...], stack_right(total))
            stacked = jnp.concatenate([logits[:, :256], logits[:, 256:]], axis=0)
            for u in range(2):
                abuf[hb, u * 128 : (u + 1) * 128, :] = stacked[:, u * 128 : (u + 1) * 128].T
        if hb < 3:
            to_line(
                A2Z + hb,
                lambda zz: abuf.at[hb, pl.ds(pl.multiple_of(zz * 32, 32), 32), :],
                a2m.at[hb, z],
            )
        else:
            mirror(hb, lambda zz: abuf.at[hb, pl.ds(pl.multiple_of(zz * 32, 32), 32), :], True)
        to_plane(
            A1 + hb,
            lambda qq: abuf.at[hb, pl.ds(pl.multiple_of(qq * 16, 16), 16), :],
            a1.at[hb, q],
        )

    own = lax.rem(q, 2) == q // 8
    own_direct = 2 * z + q // 8 == q

    def mirror(hb, source, direct):
        def step(k, carry):
            zz = lax.rem(z + k, NZ)
            plane = zz if direct else z
            peer = 2 * (z if direct else zz) + q // 8
            here = jnp.logical_and(plane == z, peer == q)

            @pl.when(jnp.logical_not(here))
            def _():
                remote(A2Q + hb, source(zz), a2f.at[hb, target, :], plane, peer)

            @pl.when(here)
            def _():
                local(A2Q + hb, source(zz), a2f.at[hb, target, :])

            return carry

        lax.fori_loop(0, NZ, step, 0)

    def mirror_relay(hb):
        landed(A2Z + hb, a2m.at[hb])
        mirror(hb, lambda zz: a2m.at[hb, zz], False)

    landed(PROD, prb.at[0])
    transition(0, 0)
    transition(0, 1)
    landed(PROD + 1, prb.at[1])
    transition(1, 0)
    mirror_relay(0)
    mirror_relay(1)
    transition(1, 1)
    mirror_relay(2)

    for hb in range(4):
        landed(A1 + hb, a1.at[hb])
        landed(A2Q + hb, a2f.at[hb])

    both_bias = jnp.concatenate([bias[...], bias[...]], axis=1)

    def final_step(m, carry):
        a, t = m // 8, lax.rem(m, 8)
        for b in range(2):
            for bj in range(2):
                mine = [a1[h * 2 + b, m, bj * 8 : bj * 8 + 8, :] + both_bias for h in range(2)]
                other = [a2f[hj * 2 + bj, pl.ds(a * 16 + b * 8 + t, 8, stride=32), :] for hj in range(2)]
                values = (
                    (mine[0] + other[0], pltpu.roll(mine[0], 64, 1) + other[1]),
                    (mine[1] + pltpu.roll(other[0], 64, 1), pltpu.roll(mine[1] + other[1], 64, 1)),
                )
                for h in range(2):
                    i = a * 32 + h * 16 + b * 8 + t
                    for hj in range(2):
                        j = hj * 16 + bj * 8
                        out[i, j : j + 8, :] = values[h][hj][:, :64]
        return carry

    with jax.named_scope("final"):
        lax.fori_loop(0, NQ, final_step, 0)

    for index in range(4):
        sent(LR + index, rb.at[index, pl.ds(0, ND - 1)])
    sent(BASE, base.at[pl.ds(0, NQ - 1)])
    for h in range(2):
        sent(PROD + h, psb.at[h, pl.ds(0, 8 * (ND - 1)), :])
    for hb in range(4):
        sent(A1 + hb, a1.at[hb, pl.ds(0, NQ - 1)])
        if hb < 3:
            sent(A2Z + hb, a2m.at[hb, pl.ds(0, NZ - 1)])
        kept = own if hb < 3 else own_direct

        @pl.when(kept)
        def _():
            sent(A2Q + hb, a2m.at[hb, pl.ds(0, NZ - 1)])

        @pl.when(jnp.logical_not(kept))
        def _():
            sent(A2Q + hb, a2m.at[hb])


def shards(pair, gain_in, w_in, w_gate, w_out, gain_prod, gain_trans, w_ti, w_to, w_dist, bias):
    vmem = pl.BlockSpec(memory_space=pltpu.VMEM)
    result = pl.pallas_call(
        kernel,
        out_shape=jax.ShapeDtypeStruct((64, 32, 64), F32),
        in_specs=[vmem] * 11,
        out_specs=vmem,
        scratch_shapes=[
            pltpu.VMEM((512, 384), BF),
            pltpu.VMEM((128, 384), BF),
            pltpu.VMEM((128, 384), BF),
            pltpu.VMEM((1024, 384), BF),
            pltpu.VMEM((128, 1536), BF),
            pltpu.VMEM((64, 384), BF),
            pltpu.VMEM((4, 384, 512), BF),
            pltpu.VMEM((4, ND * 8, 128), F32),
            pltpu.VMEM((4, ND, 8, 128), F32),
            pltpu.VMEM((16, 4, 32, 128), F32),
            pltpu.VMEM((4, 128, 512), F32),
            pltpu.VMEM((4, 128, 512), F32),
            pltpu.VMEM((512, 512), BF),
            pltpu.VMEM((512, 512), BF),
            pltpu.VMEM((256, 512), BF),
            pltpu.VMEM((256, 512), BF),
            pltpu.VMEM((2, ND * 8, 128), F32),
            pltpu.VMEM((2, ND * 8, 128), F32),
            pltpu.VMEM((4, 256, 128), F32),
            pltpu.VMEM((4, 16, 16, 128), F32),
            pltpu.VMEM((4, 8, 32, 128), F32),
            pltpu.VMEM((4, 256, 128), F32),
            pltpu.SemaphoreType.DMA((PHASES,)),
            pltpu.SemaphoreType.DMA((PHASES,)),
            pltpu.SemaphoreType.REGULAR,
        ],
        compiler_params=pltpu.CompilerParams(
            collective_id=0, has_side_effects=True, vmem_limit_bytes=56 * 1024 * 1024
        ),
        name="triangle",
    )(
        pair.reshape(2, 4, 8, 32, 128),
        gain_in.reshape(1, 128),
        w_in,
        w_gate,
        w_out,
        gain_prod.reshape(1, 128),
        gain_trans.reshape(1, 128),
        w_ti,
        w_to,
        w_dist.T,
        bias.reshape(1, 64),
    )
    return result.reshape(1, 64, 32, 64)


def solution(mesh):
    return jax.shard_map(
        shards,
        mesh=mesh,
        in_specs=(P("crop", "row", "col", None), P(), P(), P(), P(), P(), P(), P(), P(), P(), P()),
        out_specs=P("crop", "row", "col", None),
        check_vma=False,
    )
```

```python
import jax
import jax.numpy as jnp
from jax import lax
from jax.experimental import pallas as pl
from jax.experimental.pallas import tpu as pltpu
from jax.sharding import PartitionSpec as P

MESH = pl.DeviceIdType.MESH
BF = jnp.bfloat16
F32 = jnp.float32
NZ = 8
NQ = 16
ND = NZ * NQ

LR, BASE, PROD, A1, A2, PHASES = 0, 4, 5, 7, 11, 15
AROUND = (1, 7, 2, 6, 3, 5, 4)


def split(values):
    high = values.astype(BF)
    return high, (values - high.astype(F32)).astype(BF)


def stack_right(values):
    high, low = split(values)
    return jnp.concatenate([high, low, high], axis=0)


def normalize(values):
    center = values - jnp.mean(values, axis=0, keepdims=True)
    spread = jnp.mean(center * center, axis=0, keepdims=True)
    return center * lax.rsqrt(spread + 1e-05)


def dot(left, right):
    return lax.dot_general(left, right, (((1,), (0,)), ((), ())), preferred_element_type=F32)


def dot_nt(left, right):
    return lax.dot_general(left, right, (((1,), (1,)), ((), ())), preferred_element_type=F32)


def sigmoid(values):
    return 1.0 / (1.0 + jnp.exp(-values))


def store_weights(target, row, weights, gain, turn=True):
    depth = weights.shape[0] if turn else 128
    for part in range(depth // 128):
        turned = weights[part * 128 : (part + 1) * 128, :].T if turn else weights
        if gain is not None:
            turned = turned * gain
        high, low = split(turned)
        rows = pl.ds(row, turned.shape[0])
        at = part * 128
        target[rows, at : at + 128] = high
        target[rows, depth + at : depth + at + 128] = high
        target[rows, 2 * depth + at : 2 * depth + at + 128] = low


def kernel(
    pair_hbm,
    gain_in,
    w_in_hbm,
    w_gate_hbm,
    w_out_hbm,
    gain_prod,
    gain_trans,
    w_ti_hbm,
    w_to_hbm,
    w_dist_hbm,
    a1,
    a2f,
    pair,
    w_in,
    w_gate,
    w_out,
    w_ti,
    w_to,
    w_dist,
    win3,
    wgate3,
    wout3,
    wti3,
    wto3,
    wdist3,
    x3,
    sb,
    rb,
    base,
    xt,
    gate,
    right_high,
    right_low,
    left_high,
    left_low,
    psb,
    prb,
    abuf,
    send_sem,
    recv_sem,
    line_sem,
    load_sem,
):
    crop = lax.axis_index("crop")
    z = lax.axis_index("row")
    q = lax.axis_index("col")
    me = z * NQ + q

    def remote(phase, source, target, zz, qq):
        pltpu.make_async_remote_copy(
            src_ref=source,
            dst_ref=target,
            send_sem=send_sem.at[phase],
            recv_sem=recv_sem.at[phase],
            device_id=(crop, zz, qq),
            device_id_type=MESH,
        ).start()

    def local(phase, source, target):
        pltpu.make_async_copy(source, target, recv_sem.at[phase]).start()

    def to_all(phase, source, target, beside=None):
        with jax.named_scope("issue_%d" % phase):
            for k in AROUND:
                zz = lax.rem(z + k, NZ)
                remote(phase, source(zz * NQ + q), target, zz, q)

            def step(k, carry):
                qq = lax.rem(q + k, NQ)
                for kz in AROUND + (0,):
                    zz = lax.rem(z + kz, NZ)
                    remote(phase, source(zz * NQ + qq), target, zz, qq)
                if beside is not None:
                    beside(qq)
                return carry

            lax.fori_loop(1, NQ, step, 0)
            local(phase, source(me), target)

    def to_plane(phase, source, target):
        def step(k, carry):
            qq = lax.rem(q + k, NQ)
            remote(phase, source(qq), target, z, qq)
            return carry

        lax.fori_loop(1, NQ, step, 0)
        local(phase, source(q), target)

    def landed(phase, whole):
        with jax.named_scope("wait_%d" % phase):
            pltpu.make_async_copy(whole, whole, recv_sem.at[phase]).wait()

    def sent(phase, most):
        pltpu.make_async_copy(most, most, send_sem.at[phase]).wait()

    barrier = pltpu.get_barrier_semaphore()

    def greet_plane(k, carry):
        pl.semaphore_signal(barrier, inc=1, device_id=(crop, z, lax.rem(q + k, NQ)), device_id_type=MESH)
        return carry

    lax.fori_loop(1, NQ, greet_plane, 0)
    for k in range(1, NZ):
        pl.semaphore_signal(barrier, inc=1, device_id=(crop, lax.rem(z + k, NZ), q), device_id_type=MESH)

    loads = [
        pltpu.make_async_copy(source, target, load_sem.at[n])
        for n, (source, target) in enumerate(
            (
                (w_in_hbm, w_in),
                (pair_hbm, pair),
                (w_gate_hbm, w_gate),
                (w_out_hbm, w_out),
                (w_ti_hbm, w_ti),
                (w_to_hbm, w_to),
                (w_dist_hbm, w_dist),
            )
        )
    ]
    for load in loads:
        load.start()

    def input_weights(blocks):
        for block in blocks:
            store_weights(win3, block * 128, w_in[:, block * 128 : (block + 1) * 128], gain_in[...])

    with jax.named_scope("load_first"):
        loads[0].wait()
        input_weights((2, 3))
        loads[1].wait()

    def norm_chunk(h):
        def step(n, carry):
            blocks = []
            for u in range(4):
                rows = pair[:, h * 2 : h * 2 + 2, n * 4 + u, :, :]
                blocks.append(rows.reshape(128, 128).T)
            x3[h * 2 + n] = stack_right(normalize(jnp.concatenate(blocks, axis=1)))
            return carry

        with jax.named_scope("norm"):
            lax.fori_loop(0, 2, step, 0)

    def project_chunk(side, h):
        first = 256 if side == 0 else 0
        index = side * 2 + h

        def step(n, carry):
            both = dot(win3[first : first + 256, :], x3[h * 2 + n])
            value = sigmoid(both[128:, :]) * both[:128, :]
            for u in range(4):
                sb[index, pl.ds(n * 4 + u, 128, stride=8), :] = value[:, u * 128 : (u + 1) * 128]
            return carry

        with jax.named_scope("project"):
            lax.fori_loop(0, 2, step, 0)

    def send_chunk(index, beside=None):
        to_all(
            LR + index,
            lambda p: sb.at[index, pl.ds(pl.multiple_of(p * 8, 8), 8), :],
            rb.at[index, me],
            beside,
        )

    def pair_source(peer):
        return pair.at[lax.rem(peer, 2), :, peer // 2]

    def send_first():
        source = lambda p: sb.at[0, pl.ds(pl.multiple_of(p * 8, 8), 8), :]
        target = rb.at[0, me]
        for k in AROUND:
            zz = lax.rem(z + k, NZ)
            with jax.named_scope("wait_line"):
                pl.semaphore_wait(line_sem.at[k], 1)

            def step(kq, carry):
                qq = lax.rem(q + kq, NQ)
                remote(LR, source(zz * NQ + qq), target, zz, qq)
                return carry

            lax.fori_loop(0, NQ, step, 0)

        def plane_step(kq, carry):
            qq = lax.rem(q + kq, NQ)
            remote(LR, source(z * NQ + qq), target, z, qq)
            return carry

        lax.fori_loop(1, NQ, plane_step, 0)
        local(LR, source(me), target)

    norm_chunk(0)
    project_chunk(0, 0)
    with jax.named_scope("wait_barrier"):
        pl.semaphore_wait(barrier, NQ - 1 + NZ - 1)
    for k in range(1, NZ):
        pl.semaphore_signal(
            line_sem.at[NZ - k], inc=1, device_id=(crop, lax.rem(z + k, NZ), q), device_id_type=MESH
        )
    send_first()
    norm_chunk(1)
    project_chunk(0, 1)
    send_chunk(1)
    input_weights((0, 1))
    project_chunk(1, 0)
    send_chunk(2, lambda qq: remote(BASE, pair_source(qq), base.at[q], z, qq))
    local(BASE, pair_source(q), base.at[q])
    project_chunk(1, 1)
    send_chunk(3)

    with jax.named_scope("weights"):
        for load in loads[2:]:
            load.wait()
        store_weights(wgate3, 0, w_gate[...], gain_in[...])
        store_weights(wout3, 0, w_out[...], gain_prod[...])
        for block in range(8):
            store_weights(wti3, block * 128, w_ti[:, block * 128 : (block + 1) * 128], gain_trans[...])
        store_weights(wto3, 0, w_to[...], None)
        store_weights(wdist3, 0, w_dist[...], None, turn=False)

    lane = lax.broadcasted_iota(jnp.int32, (8, 128), 1)
    low_half = lane < 64
    even_block = lax.rem(lane, 64) < 32

    def assemble(index, high_ref, low_ref, first):
        landed(LR + index, rb.at[index])

        def step(zz, carry):
            for group in range(4):
                v = [rb[index, zz * NQ + group * 4 + u] for u in range(4)]
                s = [None] * 4
                for u in range(2):
                    s[u] = jnp.where(low_half, v[u], pltpu.roll(v[u + 2], 64, 1))
                    s[u + 2] = jnp.where(low_half, pltpu.roll(v[u], 64, 1), v[u + 2])
                for a in range(2):
                    even, odd = s[2 * a], s[2 * a + 1]
                    both = jnp.concatenate(
                        [
                            jnp.where(even_block, even, pltpu.roll(odd, 32, 1)),
                            jnp.where(even_block, pltpu.roll(even, 96, 1), odd),
                        ],
                        axis=0,
                    )
                    high, low = split(both)
                    rows = pl.ds(pl.multiple_of(first + zz * 32 + a * 16, 16), 16)
                    high_ref[rows, group * 128 : (group + 1) * 128] = high
                    low_ref[rows, group * 128 : (group + 1) * 128] = low
            return carry

        with jax.named_scope("assemble"):
            lax.fori_loop(0, NZ, step, 0)

    assemble(0, right_high, right_low, 0)
    assemble(1, right_high, right_low, 256)

    def multiply(h):
        assemble(2 + h, left_high, left_low, 0)
        with jax.named_scope("product"):
            for half in range(2):
                rows = slice(half * 256, half * 256 + 256)
                product = (
                    dot_nt(left_high[...], right_high[rows, :])
                    + dot_nt(left_high[...], right_low[rows, :])
                    + dot_nt(left_low[...], right_high[rows, :])
                )
                for zz in range(NZ):
                    for a in range(2):
                        for b in range(2):
                            row = zz * 32 + a * 16 + b * 8
                            for u in range(2):
                                start = (zz * 16 + a) * 8 + b * 4 + half * 2 + u
                                psb[h, pl.ds(start, 8, stride=16), :] = product[row : row + 8, u * 128 : (u + 1) * 128]
        to_all(
            PROD + h,
            lambda p: psb.at[h, pl.ds(pl.multiple_of(p * 8, 8), 8), :],
            prb.at[h, pl.ds(pl.multiple_of(me * 8, 8), 8), :],
        )

    multiply(0)
    landed(BASE, base)

    def base_step(hb, carry):
        blocks = []
        for jt in range(4):
            some = base[(jt % 2) * 8 : (jt % 2) * 8 + 8, hb, (jt // 2) * 16 : (jt // 2) * 16 + 16, :]
            blocks.append(some.reshape(128, 128).T)
        value = jnp.concatenate(blocks, axis=1)
        xt[hb] = value
        gate[hb] = sigmoid(dot(wgate3[...], stack_right(normalize(value))))
        return carry

    with jax.named_scope("base_gate"):
        lax.fori_loop(0, 4, base_step, 0)
    multiply(1)

    def transition(h, b):
        hb = h * 2 + b
        with jax.named_scope("transition"):
            product = jnp.concatenate(
                [prb[h, pl.ds(b * 4 + jt, 128, stride=8), :] for jt in range(4)], axis=1
            )
            updated = xt[hb] + gate[hb] * dot(wout3[...], stack_right(normalize(product)))
            right = stack_right(normalize(updated))
            total = updated
            for part in range(2):
                at = part * 256
                up_gate = dot(wti3[at : at + 256, :], right)
                up = dot(wti3[512 + at : 768 + at, :], right)
                high, low = split(up_gate * sigmoid(up_gate) * up)
                total = total + dot(wto3[:, at : at + 256], high)
                total = total + dot(wto3[:, 512 + at : 768 + at], low)
                total = total + dot(wto3[:, 1024 + at : 1280 + at], high)
            logits = dot(wdist3[...], stack_right(total))
            stacked = jnp.concatenate([logits[:, :256], logits[:, 256:]], axis=0)
            for u in range(2):
                abuf[hb, u * 128 : (u + 1) * 128, :] = stacked[:, u * 128 : (u + 1) * 128].T
        mirror(hb)
        to_plane(
            A1 + hb,
            lambda qq: abuf.at[hb, pl.ds(pl.multiple_of(qq * 16, 16), 16), :],
            a1.at[hb, q // 2, lax.rem(q, 2)],
        )

    twin = 2 * z + lax.rem(q, 2)

    def mirror(hb):
        target = a2f.at[hb, q // 2]
        for k in AROUND:
            zz = lax.rem(z + k, NZ)
            remote(A2 + hb, abuf.at[hb, pl.ds(pl.multiple_of(zz * 32, 32), 32), :], target, zz, twin)
        source = abuf.at[hb, pl.ds(pl.multiple_of(z * 32, 32), 32), :]

        @pl.when(twin != q)
        def _():
            remote(A2 + hb, source, target, z, twin)

        @pl.when(twin == q)
        def _():
            local(A2 + hb, source, target)

    landed(PROD, prb.at[0])
    transition(0, 0)
    transition(0, 1)
    landed(PROD + 1, prb.at[1])
    transition(1, 0)
    transition(1, 1)

    for hb in range(4):
        landed(A1 + hb, a1.at[hb])
        landed(A2 + hb, a2f.at[hb])

    for index in range(4):
        sent(LR + index, rb.at[index, pl.ds(0, ND - 1)])
    sent(BASE, base.at[pl.ds(0, NQ - 1)])
    for h in range(2):
        sent(PROD + h, psb.at[h, pl.ds(0, 8 * (ND - 1)), :])
    for hb in range(4):
        sent(A1 + hb, abuf.at[hb, pl.ds(0, 16 * (NQ - 1)), :])

        @pl.when(twin == q)
        def _():
            sent(A2 + hb, abuf.at[hb, pl.ds(0, 32 * (NZ - 1)), :])

        @pl.when(twin != q)
        def _():
            sent(A2 + hb, abuf.at[hb])


def add_mirrored(a1, a2f, bias, out):
    both_bias = jnp.concatenate([bias[...], bias[...]], axis=1)
    for b in range(2):
        for bj in range(2):
            for t in range(8):
                mine = [a1[h * 2 + b, t, 0, bj * 8 : bj * 8 + 8, :] + both_bias for h in range(2)]
                other = [a2f[hj * 2 + bj, :, b * 8 + t, :] for hj in range(2)]
                values = (
                    (mine[0] + other[0], pltpu.roll(mine[0], 64, 1) + other[1]),
                    (mine[1] + pltpu.roll(other[0], 64, 1), pltpu.roll(mine[1] + other[1], 64, 1)),
                )
                for h in range(2):
                    for hj in range(2):
                        j = hj * 16 + bj * 8
                        out[h * 16 + b * 8 + t, j : j + 8, :] = values[h][hj][:, :64]


def shards(pair, gain_in, w_in, w_gate, w_out, gain_prod, gain_trans, w_ti, w_to, w_dist, bias):
    vmem = pl.BlockSpec(memory_space=pltpu.VMEM)
    hbm = pl.BlockSpec(memory_space=pl.ANY)
    own, mirrored = pl.pallas_call(
        kernel,
        out_shape=(
            jax.ShapeDtypeStruct((4, 8, 2, 16, 128), F32),
            jax.ShapeDtypeStruct((4, 8, 32, 128), F32),
        ),
        in_specs=[hbm, vmem, hbm, hbm, hbm, vmem, vmem, hbm, hbm, hbm],
        out_specs=(hbm, hbm),
        scratch_shapes=[
            pltpu.VMEM((2, 4, 8, 32, 128), F32),
            pltpu.VMEM((128, 512), F32),
            pltpu.VMEM((128, 128), F32),
            pltpu.VMEM((128, 128), F32),
            pltpu.VMEM((128, 1024), F32),
            pltpu.VMEM((512, 128), F32),
            pltpu.VMEM((64, 128), F32),
            pltpu.VMEM((512, 384), BF),
            pltpu.VMEM((128, 384), BF),
            pltpu.VMEM((128, 384), BF),
            pltpu.VMEM((1024, 384), BF),
            pltpu.VMEM((128, 1536), BF),
            pltpu.VMEM((64, 384), BF),
            pltpu.VMEM((4, 384, 512), BF),
            pltpu.VMEM((4, ND * 8, 128), F32),
            pltpu.VMEM((4, ND, 8, 128), F32),
            pltpu.VMEM((16, 4, 32, 128), F32),
            pltpu.VMEM((4, 128, 512), F32),
            pltpu.VMEM((4, 128, 512), F32),
            pltpu.VMEM((512, 512), BF),
            pltpu.VMEM((512, 512), BF),
            pltpu.VMEM((256, 512), BF),
            pltpu.VMEM((256, 512), BF),
            pltpu.VMEM((2, ND * 8, 128), F32),
            pltpu.VMEM((2, ND * 8, 128), F32),
            pltpu.VMEM((4, 256, 128), F32),
            pltpu.SemaphoreType.DMA((PHASES,)),
            pltpu.SemaphoreType.DMA((PHASES,)),
            pltpu.SemaphoreType.REGULAR((NZ,)),
            pltpu.SemaphoreType.DMA((7,)),
        ],
        compiler_params=pltpu.CompilerParams(
            collective_id=0, has_side_effects=True, vmem_limit_bytes=56 * 1024 * 1024
        ),
        name="triangle",
    )(
        pair.reshape(2, 4, 8, 32, 128),
        gain_in.reshape(1, 128),
        w_in,
        w_gate,
        w_out,
        gain_prod.reshape(1, 128),
        gain_trans.reshape(1, 128),
        w_ti,
        w_to,
        w_dist.T,
    )
    result = pl.pallas_call(
        add_mirrored,
        grid=(2,),
        out_shape=jax.ShapeDtypeStruct((64, 32, 64), F32),
        in_specs=[
            pl.BlockSpec((4, 8, 1, 16, 128), lambda a: (0, 0, a, 0, 0)),
            pl.BlockSpec((4, 8, 16, 128), lambda a: (0, 0, a, 0)),
            pl.BlockSpec((1, 64), lambda a: (0, 0)),
        ],
        out_specs=pl.BlockSpec((32, 32, 64), lambda a: (a, 0, 0)),
        name="add_mirrored",
    )(own, mirrored, bias.reshape(1, 64))
    return result.reshape(1, 64, 32, 64)


def solution(mesh):
    return jax.shard_map(
        shards,
        mesh=mesh,
        in_specs=(P("crop", "row", "col", None), P(), P(), P(), P(), P(), P(), P(), P(), P(), P()),
        out_specs=P("crop", "row", "col", None),
        check_vma=False,
    )
```

```python
import jax
import jax.numpy as jnp
from jax import lax
from jax.experimental import pallas as pl
from jax.experimental.pallas import tpu as pltpu
from jax.sharding import PartitionSpec as P

MESH = pl.DeviceIdType.MESH
BF = jnp.bfloat16
F32 = jnp.float32
NZ = 8
NQ = 16
ND = NZ * NQ

LR, BASE, PROD, A1, A2, PHASES = 0, 4, 5, 7, 11, 15
AROUND = (1, 7, 2, 6, 3, 5, 4)


def split(values):
    high = values.astype(BF)
    return high, (values - high.astype(F32)).astype(BF)


def stack_right(values):
    high, low = split(values)
    return jnp.concatenate([high, low, high], axis=0)


def normalize(values):
    center = values - jnp.mean(values, axis=0, keepdims=True)
    spread = jnp.mean(center * center, axis=0, keepdims=True)
    return center * lax.rsqrt(spread + 1e-05)


def dot(left, right):
    return lax.dot_general(left, right, (((1,), (0,)), ((), ())), preferred_element_type=F32)


def dot_nt(left, right):
    return lax.dot_general(left, right, (((1,), (1,)), ((), ())), preferred_element_type=F32)


def sigmoid(values):
    return 1.0 / (1.0 + jnp.exp(-values))


def store_weights(target, row, weights, gain, turn=True):
    depth = weights.shape[0] if turn else 128
    for part in range(depth // 128):
        turned = weights[part * 128 : (part + 1) * 128, :].T if turn else weights
        if gain is not None:
            turned = turned * gain
        high, low = split(turned)
        rows = pl.ds(row, turned.shape[0])
        at = part * 128
        target[rows, at : at + 128] = high
        target[rows, depth + at : depth + at + 128] = high
        target[rows, 2 * depth + at : 2 * depth + at + 128] = low


def kernel(
    pair_hbm,
    gain_in_hbm,
    w_in_hbm,
    w_gate_hbm,
    w_out_hbm,
    gain_prod_hbm,
    gain_trans_hbm,
    w_ti_hbm,
    w_to_hbm,
    w_dist_hbm,
    a1,
    a2f,
    pair,
    w_in,
    w_gate,
    w_out,
    w_ti,
    w_to,
    w_dist,
    gain_in,
    gain_prod,
    gain_trans,
    win3,
    wgate3,
    wout3,
    wti3,
    wto3,
    wdist3,
    x3,
    sb,
    rb,
    base,
    xt,
    gate,
    right_high,
    right_low,
    left_high,
    left_low,
    psb,
    prb,
    abuf,
    send_sem,
    recv_sem,
    line_sem,
    load_sem,
):
    crop = lax.axis_index("crop")
    z = lax.axis_index("row")
    q = lax.axis_index("col")
    me = z * NQ + q

    def remote(phase, source, target, zz, qq):
        pltpu.make_async_remote_copy(
            src_ref=source,
            dst_ref=target,
            send_sem=send_sem.at[phase],
            recv_sem=recv_sem.at[phase],
            device_id=(crop, zz, qq),
            device_id_type=MESH,
        ).start()

    def local(phase, source, target):
        pltpu.make_async_copy(source, target, recv_sem.at[phase]).start()

    def to_all(phase, source, target, beside=None):
        with jax.named_scope("issue_%d" % phase):
            for k in AROUND:
                zz = lax.rem(z + k, NZ)
                remote(phase, source(zz * NQ + q), target, zz, q)

            def step(k, carry):
                qq = lax.rem(q + k, NQ)
                for kz in AROUND + (0,):
                    zz = lax.rem(z + kz, NZ)
                    remote(phase, source(zz * NQ + qq), target, zz, qq)
                if beside is not None:
                    beside(qq)
                return carry

            lax.fori_loop(1, NQ, step, 0)
            local(phase, source(me), target)

    def to_plane(phase, source, target):
        def step(k, carry):
            qq = lax.rem(q + k, NQ)
            remote(phase, source(qq), target, z, qq)
            return carry

        lax.fori_loop(1, NQ, step, 0)
        local(phase, source(q), target)

    def landed(phase, whole):
        with jax.named_scope("wait_%d" % phase):
            pltpu.make_async_copy(whole, whole, recv_sem.at[phase]).wait()

    def sent(phase, most):
        pltpu.make_async_copy(most, most, send_sem.at[phase]).wait()

    loads = [
        pltpu.make_async_copy(source, target, load_sem.at[n])
        for n, (source, target) in enumerate(
            (
                (gain_in_hbm, gain_in),
                (w_in_hbm.at[:, 256:512], w_in.at[:, 256:512]),
                (pair_hbm.at[:, 0:2], pair.at[:, 0:2]),
                (pair_hbm.at[:, 2:4], pair.at[:, 2:4]),
                (w_in_hbm.at[:, 0:256], w_in.at[:, 0:256]),
                (w_gate_hbm, w_gate),
                (w_out_hbm, w_out),
                (gain_prod_hbm, gain_prod),
                (gain_trans_hbm, gain_trans),
                (w_ti_hbm, w_ti),
                (w_to_hbm, w_to),
                (w_dist_hbm, w_dist),
            )
        )
    ]
    for load in loads[:3]:
        load.start()

    barrier = pltpu.get_barrier_semaphore()

    def greet_plane(k, carry):
        pl.semaphore_signal(barrier, inc=1, device_id=(crop, z, lax.rem(q + k, NQ)), device_id_type=MESH)
        return carry

    lax.fori_loop(1, NQ, greet_plane, 0)
    for k in range(1, NZ):
        pl.semaphore_signal(barrier, inc=1, device_id=(crop, lax.rem(z + k, NZ), q), device_id_type=MESH)

    def input_weights(blocks):
        for block in blocks:
            store_weights(win3, block * 128, w_in[:, block * 128 : (block + 1) * 128], gain_in[...])

    with jax.named_scope("load_first"):
        loads[0].wait()
        loads[1].wait()
        input_weights((2, 3))
        loads[2].wait()
    for load in loads[3:]:
        load.start()

    def norm_chunk(h):
        def step(n, carry):
            blocks = []
            for u in range(4):
                rows = pair[:, h * 2 : h * 2 + 2, n * 4 + u, :, :]
                blocks.append(rows.reshape(128, 128).T)
            x3[h * 2 + n] = stack_right(normalize(jnp.concatenate(blocks, axis=1)))
            return carry

        with jax.named_scope("norm"):
            lax.fori_loop(0, 2, step, 0)

    def project_chunk(side, h):
        first = 256 if side == 0 else 0
        index = side * 2 + h

        def step(n, carry):
            both = dot(win3[first : first + 256, :], x3[h * 2 + n])
            value = sigmoid(both[128:, :]) * both[:128, :]
            for u in range(4):
                sb[index, pl.ds(n * 4 + u, 128, stride=8), :] = value[:, u * 128 : (u + 1) * 128]
            return carry

        with jax.named_scope("project"):
            lax.fori_loop(0, 2, step, 0)

    def send_chunk(index, beside=None):
        to_all(
            LR + index,
            lambda p: sb.at[index, pl.ds(pl.multiple_of(p * 8, 8), 8), :],
            rb.at[index, me],
            beside,
        )

    def pair_source(peer):
        return pair.at[lax.rem(peer, 2), :, peer // 2]

    def send_first():
        source = lambda p: sb.at[0, pl.ds(pl.multiple_of(p * 8, 8), 8), :]
        target = rb.at[0, me]
        for k in AROUND:
            zz = lax.rem(z + k, NZ)
            with jax.named_scope("wait_line"):
                pl.semaphore_wait(line_sem.at[k], 1)

            def step(kq, carry):
                qq = lax.rem(q + kq, NQ)
                remote(LR, source(zz * NQ + qq), target, zz, qq)
                return carry

            lax.fori_loop(0, NQ, step, 0)

        def plane_step(kq, carry):
            qq = lax.rem(q + kq, NQ)
            remote(LR, source(z * NQ + qq), target, z, qq)
            return carry

        lax.fori_loop(1, NQ, plane_step, 0)
        local(LR, source(me), target)

    norm_chunk(0)
    project_chunk(0, 0)
    with jax.named_scope("wait_barrier"):
        pl.semaphore_wait(barrier, NQ - 1 + NZ - 1)
    for k in range(1, NZ):
        pl.semaphore_signal(
            line_sem.at[NZ - k], inc=1, device_id=(crop, lax.rem(z + k, NZ), q), device_id_type=MESH
        )
    send_first()
    loads[3].wait()
    norm_chunk(1)
    project_chunk(0, 1)
    send_chunk(1)
    loads[4].wait()
    input_weights((0, 1))
    project_chunk(1, 0)
    send_chunk(2, lambda qq: remote(BASE, pair_source(qq), base.at[q], z, qq))
    local(BASE, pair_source(q), base.at[q])
    project_chunk(1, 1)
    send_chunk(3)

    with jax.named_scope("weights"):
        for load in loads[5:]:
            load.wait()
        store_weights(wgate3, 0, w_gate[...], gain_in[...])
        store_weights(wout3, 0, w_out[...], gain_prod[...])
        for block in range(8):
            store_weights(wti3, block * 128, w_ti[:, block * 128 : (block + 1) * 128], gain_trans[...])
        store_weights(wto3, 0, w_to[...], None)
        store_weights(wdist3, 0, w_dist[...], None, turn=False)

    lane = lax.broadcasted_iota(jnp.int32, (8, 128), 1)
    low_half = lane < 64
    even_block = lax.rem(lane, 64) < 32

    def assemble(index, high_ref, low_ref, first):
        landed(LR + index, rb.at[index])

        def step(zz, carry):
            for group in range(4):
                v = [rb[index, zz * NQ + group * 4 + u] for u in range(4)]
                s = [None] * 4
                for u in range(2):
                    s[u] = jnp.where(low_half, v[u], pltpu.roll(v[u + 2], 64, 1))
                    s[u + 2] = jnp.where(low_half, pltpu.roll(v[u], 64, 1), v[u + 2])
                for a in range(2):
                    even, odd = s[2 * a], s[2 * a + 1]
                    both = jnp.concatenate(
                        [
                            jnp.where(even_block, even, pltpu.roll(odd, 32, 1)),
                            jnp.where(even_block, pltpu.roll(even, 96, 1), odd),
                        ],
                        axis=0,
                    )
                    high, low = split(both)
                    rows = pl.ds(pl.multiple_of(first + zz * 32 + a * 16, 16), 16)
                    high_ref[rows, group * 128 : (group + 1) * 128] = high
                    low_ref[rows, group * 128 : (group + 1) * 128] = low
            return carry

        with jax.named_scope("assemble"):
            lax.fori_loop(0, NZ, step, 0)

    assemble(0, right_high, right_low, 0)
    assemble(1, right_high, right_low, 256)

    def multiply(h):
        assemble(2 + h, left_high, left_low, 0)
        with jax.named_scope("product"):
            for half in range(2):
                rows = slice(half * 256, half * 256 + 256)
                product = (
                    dot_nt(left_high[...], right_high[rows, :])
                    + dot_nt(left_high[...], right_low[rows, :])
                    + dot_nt(left_low[...], right_high[rows, :])
                )
                for zz in range(NZ):
                    for a in range(2):
                        for b in range(2):
                            row = zz * 32 + a * 16 + b * 8
                            for u in range(2):
                                start = (zz * 16 + a) * 8 + b * 4 + half * 2 + u
                                psb[h, pl.ds(start, 8, stride=16), :] = product[row : row + 8, u * 128 : (u + 1) * 128]
        to_all(
            PROD + h,
            lambda p: psb.at[h, pl.ds(pl.multiple_of(p * 8, 8), 8), :],
            prb.at[h, pl.ds(pl.multiple_of(me * 8, 8), 8), :],
        )

    multiply(0)
    landed(BASE, base)

    def base_step(hb, carry):
        blocks = []
        for jt in range(4):
            some = base[(jt % 2) * 8 : (jt % 2) * 8 + 8, hb, (jt // 2) * 16 : (jt // 2) * 16 + 16, :]
            blocks.append(some.reshape(128, 128).T)
        value = jnp.concatenate(blocks, axis=1)
        xt[hb] = value
        gate[hb] = sigmoid(dot(wgate3[...], stack_right(normalize(value))))
        return carry

    with jax.named_scope("base_gate"):
        lax.fori_loop(0, 4, base_step, 0)
    multiply(1)

    def transition(h, b):
        hb = h * 2 + b
        with jax.named_scope("transition"):
            product = jnp.concatenate(
                [prb[h, pl.ds(b * 4 + jt, 128, stride=8), :] for jt in range(4)], axis=1
            )
            updated = xt[hb] + gate[hb] * dot(wout3[...], stack_right(normalize(product)))
            right = stack_right(normalize(updated))
            total = updated
            for part in range(2):
                at = part * 256
                up_gate = dot(wti3[at : at + 256, :], right)
                up = dot(wti3[512 + at : 768 + at, :], right)
                high, low = split(up_gate * sigmoid(up_gate) * up)
                total = total + dot(wto3[:, at : at + 256], high)
                total = total + dot(wto3[:, 512 + at : 768 + at], low)
                total = total + dot(wto3[:, 1024 + at : 1280 + at], high)
            logits = dot(wdist3[...], stack_right(total))
            stacked = jnp.concatenate([logits[:, :256], logits[:, 256:]], axis=0)
            for u in range(2):
                abuf[hb, u * 128 : (u + 1) * 128, :] = stacked[:, u * 128 : (u + 1) * 128].T
        mirror(hb)
        to_plane(
            A1 + hb,
            lambda qq: abuf.at[hb, pl.ds(pl.multiple_of(qq * 16, 16), 16), :],
            a1.at[hb, q // 2, lax.rem(q, 2)],
        )

    twin = 2 * z + lax.rem(q, 2)

    def mirror(hb):
        target = a2f.at[hb, q // 2]
        for k in AROUND:
            zz = lax.rem(z + k, NZ)
            remote(A2 + hb, abuf.at[hb, pl.ds(pl.multiple_of(zz * 32, 32), 32), :], target, zz, twin)
        source = abuf.at[hb, pl.ds(pl.multiple_of(z * 32, 32), 32), :]

        @pl.when(twin != q)
        def _():
            remote(A2 + hb, source, target, z, twin)

        @pl.when(twin == q)
        def _():
            local(A2 + hb, source, target)

    landed(PROD, prb.at[0])
    transition(0, 0)
    transition(0, 1)
    landed(PROD + 1, prb.at[1])
    transition(1, 0)
    transition(1, 1)

    for hb in range(4):
        landed(A1 + hb, a1.at[hb])
        landed(A2 + hb, a2f.at[hb])

    for index in range(4):
        sent(LR + index, rb.at[index, pl.ds(0, ND - 1)])
    sent(BASE, base.at[pl.ds(0, NQ - 1)])
    for h in range(2):
        sent(PROD + h, psb.at[h, pl.ds(0, 8 * (ND - 1)), :])
    for hb in range(4):
        sent(A1 + hb, abuf.at[hb, pl.ds(0, 16 * (NQ - 1)), :])

        @pl.when(twin == q)
        def _():
            sent(A2 + hb, abuf.at[hb, pl.ds(0, 32 * (NZ - 1)), :])

        @pl.when(twin != q)
        def _():
            sent(A2 + hb, abuf.at[hb])


def add_mirrored(a1, a2f, bias, out):
    both_bias = jnp.concatenate([bias[...], bias[...]], axis=1)
    for b in range(2):
        for bj in range(2):
            for t in range(8):
                mine = [a1[h * 2 + b, t, 0, bj * 8 : bj * 8 + 8, :] + both_bias for h in range(2)]
                other = [a2f[hj * 2 + bj, :, b * 8 + t, :] for hj in range(2)]
                values = (
                    (mine[0] + other[0], pltpu.roll(mine[0], 64, 1) + other[1]),
                    (mine[1] + pltpu.roll(other[0], 64, 1), pltpu.roll(mine[1] + other[1], 64, 1)),
                )
                for h in range(2):
                    for hj in range(2):
                        j = hj * 16 + bj * 8
                        out[h * 16 + b * 8 + t, j : j + 8, :] = values[h][hj][:, :64]


def shards(pair, gain_in, w_in, w_gate, w_out, gain_prod, gain_trans, w_ti, w_to, w_dist, bias):
    hbm = pl.BlockSpec(memory_space=pl.ANY)
    own, mirrored = pl.pallas_call(
        kernel,
        out_shape=(
            jax.ShapeDtypeStruct((4, 8, 2, 16, 128), F32),
            jax.ShapeDtypeStruct((4, 8, 32, 128), F32),
        ),
        in_specs=[hbm] * 10,
        out_specs=(hbm, hbm),
        scratch_shapes=[
            pltpu.VMEM((2, 4, 8, 32, 128), F32),
            pltpu.VMEM((128, 512), F32),
            pltpu.VMEM((128, 128), F32),
            pltpu.VMEM((128, 128), F32),
            pltpu.VMEM((128, 1024), F32),
            pltpu.VMEM((512, 128), F32),
            pltpu.VMEM((64, 128), F32),
            pltpu.VMEM((1, 128), F32),
            pltpu.VMEM((1, 128), F32),
            pltpu.VMEM((1, 128), F32),
            pltpu.VMEM((512, 384), BF),
            pltpu.VMEM((128, 384), BF),
            pltpu.VMEM((128, 384), BF),
            pltpu.VMEM((1024, 384), BF),
            pltpu.VMEM((128, 1536), BF),
            pltpu.VMEM((64, 384), BF),
            pltpu.VMEM((4, 384, 512), BF),
            pltpu.VMEM((4, ND * 8, 128), F32),
            pltpu.VMEM((4, ND, 8, 128), F32),
            pltpu.VMEM((16, 4, 32, 128), F32),
            pltpu.VMEM((4, 128, 512), F32),
            pltpu.VMEM((4, 128, 512), F32),
            pltpu.VMEM((512, 512), BF),
            pltpu.VMEM((512, 512), BF),
            pltpu.VMEM((256, 512), BF),
            pltpu.VMEM((256, 512), BF),
            pltpu.VMEM((2, ND * 8, 128), F32),
            pltpu.VMEM((2, ND * 8, 128), F32),
            pltpu.VMEM((4, 256, 128), F32),
            pltpu.SemaphoreType.DMA((PHASES,)),
            pltpu.SemaphoreType.DMA((PHASES,)),
            pltpu.SemaphoreType.REGULAR((NZ,)),
            pltpu.SemaphoreType.DMA((12,)),
        ],
        compiler_params=pltpu.CompilerParams(
            collective_id=0, has_side_effects=True, vmem_limit_bytes=56 * 1024 * 1024
        ),
        name="triangle",
    )(
        pair.reshape(2, 4, 8, 32, 128),
        gain_in.reshape(1, 128),
        w_in,
        w_gate,
        w_out,
        gain_prod.reshape(1, 128),
        gain_trans.reshape(1, 128),
        w_ti,
        w_to,
        w_dist.T,
    )
    result = pl.pallas_call(
        add_mirrored,
        grid=(2,),
        out_shape=jax.ShapeDtypeStruct((64, 32, 64), F32),
        in_specs=[
            pl.BlockSpec((4, 8, 1, 16, 128), lambda a: (0, 0, a, 0, 0)),
            pl.BlockSpec((4, 8, 16, 128), lambda a: (0, 0, a, 0)),
            pl.BlockSpec((1, 64), lambda a: (0, 0)),
        ],
        out_specs=pl.BlockSpec((32, 32, 64), lambda a: (a, 0, 0)),
        name="add_mirrored",
    )(own, mirrored, bias.reshape(1, 64))
    return result.reshape(1, 64, 32, 64)


def solution(mesh):
    return jax.shard_map(
        shards,
        mesh=mesh,
        in_specs=(P("crop", "row", "col", None), P(), P(), P(), P(), P(), P(), P(), P(), P(), P()),
        out_specs=P("crop", "row", "col", None),
        check_vma=False,
    )
```

```python
import jax
import jax.numpy as jnp
from jax import lax
from jax.experimental import pallas as pl
from jax.experimental.pallas import tpu as pltpu
from jax.sharding import PartitionSpec as P

MESH = pl.DeviceIdType.MESH
BF = jnp.bfloat16
F32 = jnp.float32
NZ = 8
NQ = 16
ND = NZ * NQ

LR, BASE, PROD, A1, A2, PHASES = 0, 4, 5, 7, 11, 15
AROUND = (1, 7, 2, 6, 3, 5, 4)


def split(values):
    high = values.astype(BF)
    return high, (values - high.astype(F32)).astype(BF)


def stack_right(values):
    high, low = split(values)
    return jnp.concatenate([high, low, high], axis=0)


def normalize(values):
    center = values - jnp.mean(values, axis=0, keepdims=True)
    spread = jnp.mean(center * center, axis=0, keepdims=True)
    return center * lax.rsqrt(spread + 1e-05)


def dot(left, right):
    return lax.dot_general(left, right, (((1,), (0,)), ((), ())), preferred_element_type=F32)


def dot_nt(left, right):
    return lax.dot_general(left, right, (((1,), (1,)), ((), ())), preferred_element_type=F32)


def sigmoid(values):
    return 1.0 / (1.0 + jnp.exp(-values))


def store_weights(target, row, weights, gain, turn=True):
    depth = weights.shape[0] if turn else 128
    for part in range(depth // 128):
        turned = weights[part * 128 : (part + 1) * 128, :].T if turn else weights
        if gain is not None:
            turned = turned * gain
        high, low = split(turned)
        rows = pl.ds(row, turned.shape[0])
        at = part * 128
        target[rows, at : at + 128] = high
        target[rows, depth + at : depth + at + 128] = high
        target[rows, 2 * depth + at : 2 * depth + at + 128] = low


def kernel(
    pair_hbm,
    gain_in_hbm,
    w_in_hbm,
    w_gate_hbm,
    w_out_hbm,
    gain_prod_hbm,
    gain_trans_hbm,
    w_ti_hbm,
    w_to_hbm,
    w_dist_hbm,
    a1,
    a2f,
    pair,
    w_in,
    w_gate,
    w_out,
    w_ti,
    w_to,
    w_dist,
    gain_in,
    gain_prod,
    gain_trans,
    win3,
    wgate3,
    wout3,
    wti3,
    wto3,
    wdist3,
    x3,
    sb,
    rb,
    base,
    xt,
    gate,
    right_high,
    right_low,
    left_high,
    left_low,
    psb,
    prb,
    abuf,
    send_sem,
    recv_sem,
    line_sem,
    load_sem,
):
    crop = lax.axis_index("crop")
    z = lax.axis_index("row")
    q = lax.axis_index("col")
    me = z * NQ + q

    def remote(phase, source, target, zz, qq):
        pltpu.make_async_remote_copy(
            src_ref=source,
            dst_ref=target,
            send_sem=send_sem.at[phase],
            recv_sem=recv_sem.at[phase],
            device_id=(crop, zz, qq),
            device_id_type=MESH,
        ).start()

    def local(phase, source, target):
        pltpu.make_async_copy(source, target, recv_sem.at[phase]).start()

    def to_all(phase, source, target, beside=None):
        with jax.named_scope("issue_%d" % phase):
            for k in AROUND:
                zz = lax.rem(z + k, NZ)
                remote(phase, source(zz * NQ + q), target, zz, q)

            def step(k, carry):
                qq = lax.rem(q + k, NQ)
                for kz in AROUND + (0,):
                    zz = lax.rem(z + kz, NZ)
                    remote(phase, source(zz * NQ + qq), target, zz, qq)
                if beside is not None:
                    beside(qq)
                return carry

            lax.fori_loop(1, NQ, step, 0)
            local(phase, source(me), target)

    def to_plane(phase, source, target):
        def step(k, carry):
            qq = lax.rem(q + k, NQ)
            remote(phase, source(qq), target, z, qq)
            return carry

        lax.fori_loop(1, NQ, step, 0)
        local(phase, source(q), target)

    def landed(phase, whole):
        with jax.named_scope("wait_%d" % phase):
            pltpu.make_async_copy(whole, whole, recv_sem.at[phase]).wait()

    def sent(phase, most):
        pltpu.make_async_copy(most, most, send_sem.at[phase]).wait()

    loads = [
        pltpu.make_async_copy(source, target, load_sem.at[n])
        for n, (source, target) in enumerate(
            (
                (gain_in_hbm, gain_in),
                (w_in_hbm.at[:, 256:512], w_in.at[:, 256:512]),
                (pair_hbm.at[:, 0:2], pair.at[:, 0:2]),
                (pair_hbm.at[:, 2:4], pair.at[:, 2:4]),
                (w_in_hbm.at[:, 0:256], w_in.at[:, 0:256]),
                (w_gate_hbm, w_gate),
                (w_out_hbm, w_out),
                (gain_prod_hbm, gain_prod),
                (gain_trans_hbm, gain_trans),
                (w_ti_hbm, w_ti),
                (w_to_hbm, w_to),
                (w_dist_hbm, w_dist),
            )
        )
    ]
    for load in loads[:3]:
        load.start()

    barrier = pltpu.get_barrier_semaphore()

    def greet_plane(k, carry):
        pl.semaphore_signal(barrier, inc=1, device_id=(crop, z, lax.rem(q + k, NQ)), device_id_type=MESH)
        return carry

    lax.fori_loop(1, NQ, greet_plane, 0)
    for k in range(1, NZ):
        pl.semaphore_signal(barrier, inc=1, device_id=(crop, lax.rem(z + k, NZ), q), device_id_type=MESH)

    def input_weights(blocks):
        for block in blocks:
            store_weights(win3, block * 128, w_in[:, block * 128 : (block + 1) * 128], gain_in[...])

    with jax.named_scope("load_first"):
        loads[0].wait()
        loads[1].wait()
        input_weights((2, 3))
        loads[2].wait()
    for load in loads[3:]:
        load.start()

    def norm_chunk(h):
        def step(n, carry):
            blocks = []
            for u in range(4):
                rows = pair[:, h * 2 : h * 2 + 2, n * 4 + u, :, :]
                blocks.append(rows.reshape(128, 128).T)
            x3[h * 2 + n] = stack_right(normalize(jnp.concatenate(blocks, axis=1)))
            return carry

        with jax.named_scope("norm"):
            lax.fori_loop(0, 2, step, 0)

    def project_chunk(side, h):
        first = 256 if side == 0 else 0
        index = side * 2 + h

        def step(n, carry):
            both = dot(win3[first : first + 256, :], x3[h * 2 + n])
            value = sigmoid(both[128:, :]) * both[:128, :]
            for u in range(4):
                sb[index, pl.ds(n * 4 + u, 128, stride=8), :] = value[:, u * 128 : (u + 1) * 128]
            return carry

        with jax.named_scope("project"):
            lax.fori_loop(0, 2, step, 0)

    def send_chunk(index, beside=None):
        to_all(
            LR + index,
            lambda p: sb.at[index, pl.ds(pl.multiple_of(p * 8, 8), 8), :],
            rb.at[index, me],
            beside,
        )

    def pair_source(peer):
        return pair.at[lax.rem(peer, 2), :, peer // 2]

    def send_first():
        source = lambda p: sb.at[0, pl.ds(pl.multiple_of(p * 8, 8), 8), :]
        target = rb.at[0, me]
        for k in AROUND:
            zz = lax.rem(z + k, NZ)
            with jax.named_scope("wait_line"):
                pl.semaphore_wait(line_sem.at[k], 1)

            def step(kq, carry):
                qq = lax.rem(q + kq, NQ)
                remote(LR, source(zz * NQ + qq), target, zz, qq)
                return carry

            lax.fori_loop(0, NQ, step, 0)

        def plane_step(kq, carry):
            qq = lax.rem(q + kq, NQ)
            remote(LR, source(z * NQ + qq), target, z, qq)
            return carry

        lax.fori_loop(1, NQ, plane_step, 0)
        local(LR, source(me), target)

    norm_chunk(0)
    project_chunk(0, 0)
    with jax.named_scope("wait_barrier"):
        pl.semaphore_wait(barrier, NQ - 1 + NZ - 1)
    for k in range(1, NZ):
        pl.semaphore_signal(
            line_sem.at[NZ - k], inc=1, device_id=(crop, lax.rem(z + k, NZ), q), device_id_type=MESH
        )
    send_first()
    loads[3].wait()
    norm_chunk(1)
    project_chunk(0, 1)
    send_chunk(1)
    loads[4].wait()
    input_weights((0, 1))
    project_chunk(1, 0)
    send_chunk(2, lambda qq: remote(BASE, pair_source(qq), base.at[q], z, qq))
    local(BASE, pair_source(q), base.at[q])
    project_chunk(1, 1)
    send_chunk(3)

    with jax.named_scope("weights"):
        for load in loads[5:]:
            load.wait()
        store_weights(wgate3, 0, w_gate[...], gain_in[...])
        store_weights(wout3, 0, w_out[...], gain_prod[...])
        for block in range(8):
            store_weights(wti3, block * 128, w_ti[:, block * 128 : (block + 1) * 128], gain_trans[...])
        store_weights(wto3, 0, w_to[...], None)
        store_weights(wdist3, 0, w_dist[...], None, turn=False)

    lane = lax.broadcasted_iota(jnp.int32, (8, 128), 1)
    low_half = lane < 64
    even_block = lax.rem(lane, 64) < 32

    def assemble(index, high_ref, low_ref, first):
        landed(LR + index, rb.at[index])

        def step(zz, carry):
            for group in range(4):
                v = [rb[index, zz * NQ + group * 4 + u] for u in range(4)]
                s = [None] * 4
                for u in range(2):
                    s[u] = jnp.where(low_half, v[u], pltpu.roll(v[u + 2], 64, 1))
                    s[u + 2] = jnp.where(low_half, pltpu.roll(v[u], 64, 1), v[u + 2])
                for a in range(2):
                    even, odd = s[2 * a], s[2 * a + 1]
                    both = jnp.concatenate(
                        [
                            jnp.where(even_block, even, pltpu.roll(odd, 32, 1)),
                            jnp.where(even_block, pltpu.roll(even, 96, 1), odd),
                        ],
                        axis=0,
                    )
                    high, low = split(both)
                    rows = pl.ds(pl.multiple_of(first + zz * 32 + a * 16, 16), 16)
                    high_ref[rows, group * 128 : (group + 1) * 128] = high
                    low_ref[rows, group * 128 : (group + 1) * 128] = low
            return carry

        with jax.named_scope("assemble"):
            lax.fori_loop(0, NZ, step, 0)

    assemble(0, right_high, right_low, 0)
    assemble(1, right_high, right_low, 256)

    def multiply(h):
        assemble(2 + h, left_high, left_low, 0)
        with jax.named_scope("product"):
            for half in range(2):
                rows = slice(half * 256, half * 256 + 256)
                product = (
                    dot_nt(left_high[...], right_high[rows, :])
                    + dot_nt(left_high[...], right_low[rows, :])
                    + dot_nt(left_low[...], right_high[rows, :])
                )
                for zz in range(NZ):
                    for a in range(2):
                        for b in range(2):
                            row = zz * 32 + a * 16 + b * 8
                            for u in range(2):
                                start = (zz * 16 + a) * 8 + b * 4 + half * 2 + u
                                psb[h, pl.ds(start, 8, stride=16), :] = product[row : row + 8, u * 128 : (u + 1) * 128]
        to_all(
            PROD + h,
            lambda p: psb.at[h, pl.ds(pl.multiple_of(p * 8, 8), 8), :],
            prb.at[h, pl.ds(pl.multiple_of(me * 8, 8), 8), :],
        )

    multiply(0)
    landed(BASE, base)

    def base_step(hb, carry):
        blocks = []
        for jt in range(4):
            some = base[(jt % 2) * 8 : (jt % 2) * 8 + 8, hb, (jt // 2) * 16 : (jt // 2) * 16 + 16, :]
            blocks.append(some.reshape(128, 128).T)
        value = jnp.concatenate(blocks, axis=1)
        xt[hb] = value
        gate[hb] = sigmoid(dot(wgate3[...], stack_right(normalize(value))))
        return carry

    with jax.named_scope("base_gate"):
        lax.fori_loop(0, 4, base_step, 0)
    multiply(1)

    def transition(h, b):
        hb = h * 2 + b
        with jax.named_scope("transition"):
            product = jnp.concatenate(
                [prb[h, pl.ds(b * 4 + jt, 128, stride=8), :] for jt in range(4)], axis=1
            )
            updated = xt[hb] + gate[hb] * dot(wout3[...], stack_right(normalize(product)))
            right = stack_right(normalize(updated))
            total = updated
            for part in range(2):
                at = part * 256
                up_gate = dot(wti3[at : at + 256, :], right)
                up = dot(wti3[512 + at : 768 + at, :], right)
                high, low = split(up_gate / (1.0 + jnp.exp(-up_gate)) * up)
                total = total + dot(wto3[:, at : at + 256], high)
                total = total + dot(wto3[:, 512 + at : 768 + at], low)
                total = total + dot(wto3[:, 1024 + at : 1280 + at], high)
            logits = dot(wdist3[...], stack_right(total))
            stacked = jnp.concatenate([logits[:, :256], logits[:, 256:]], axis=0)
            for u in range(2):
                abuf[hb, u * 128 : (u + 1) * 128, :] = stacked[:, u * 128 : (u + 1) * 128].T
        mirror(hb)

    def own_logits(hb):
        to_plane(
            A1 + hb,
            lambda qq: abuf.at[hb, pl.ds(pl.multiple_of(qq * 16, 16), 16), :],
            a1.at[hb, q // 2, lax.rem(q, 2)],
        )

    twin = 2 * z + lax.rem(q, 2)

    def mirror(hb):
        target = a2f.at[hb, q // 2]
        for k in AROUND:
            zz = lax.rem(z + k, NZ)
            remote(A2 + hb, abuf.at[hb, pl.ds(pl.multiple_of(zz * 32, 32), 32), :], target, zz, twin)
        source = abuf.at[hb, pl.ds(pl.multiple_of(z * 32, 32), 32), :]

        @pl.when(twin != q)
        def _():
            remote(A2 + hb, source, target, z, twin)

        @pl.when(twin == q)
        def _():
            local(A2 + hb, source, target)

    landed(PROD, prb.at[0])
    transition(0, 0)
    own_logits(0)
    transition(0, 1)
    own_logits(1)
    landed(PROD + 1, prb.at[1])
    transition(1, 0)
    transition(1, 1)
    own_logits(2)
    own_logits(3)

    for hb in range(4):
        landed(A1 + hb, a1.at[hb])
        landed(A2 + hb, a2f.at[hb])

    for index in range(4):
        sent(LR + index, rb.at[index, pl.ds(0, ND - 1)])
    sent(BASE, base.at[pl.ds(0, NQ - 1)])
    for h in range(2):
        sent(PROD + h, psb.at[h, pl.ds(0, 8 * (ND - 1)), :])
    for hb in range(4):
        sent(A1 + hb, abuf.at[hb, pl.ds(0, 16 * (NQ - 1)), :])

        @pl.when(twin == q)
        def _():
            sent(A2 + hb, abuf.at[hb, pl.ds(0, 32 * (NZ - 1)), :])

        @pl.when(twin != q)
        def _():
            sent(A2 + hb, abuf.at[hb])


def add_mirrored(a1, a2f, bias, out):
    both_bias = jnp.concatenate([bias[...], bias[...]], axis=1)
    for b in range(2):
        for bj in range(2):
            for t in range(8):
                mine = [a1[h * 2 + b, t, 0, bj * 8 : bj * 8 + 8, :] + both_bias for h in range(2)]
                other = [a2f[hj * 2 + bj, :, b * 8 + t, :] for hj in range(2)]
                values = (
                    (mine[0] + other[0], pltpu.roll(mine[0], 64, 1) + other[1]),
                    (mine[1] + pltpu.roll(other[0], 64, 1), pltpu.roll(mine[1] + other[1], 64, 1)),
                )
                for h in range(2):
                    for hj in range(2):
                        j = hj * 16 + bj * 8
                        out[h * 16 + b * 8 + t, j : j + 8, :] = values[h][hj][:, :64]


def shards(pair, gain_in, w_in, w_gate, w_out, gain_prod, gain_trans, w_ti, w_to, w_dist, bias):
    hbm = pl.BlockSpec(memory_space=pl.ANY)
    own, mirrored = pl.pallas_call(
        kernel,
        out_shape=(
            jax.ShapeDtypeStruct((4, 8, 2, 16, 128), F32),
            jax.ShapeDtypeStruct((4, 8, 32, 128), F32),
        ),
        in_specs=[hbm] * 10,
        out_specs=(hbm, hbm),
        scratch_shapes=[
            pltpu.VMEM((2, 4, 8, 32, 128), F32),
            pltpu.VMEM((128, 512), F32),
            pltpu.VMEM((128, 128), F32),
            pltpu.VMEM((128, 128), F32),
            pltpu.VMEM((128, 1024), F32),
            pltpu.VMEM((512, 128), F32),
            pltpu.VMEM((64, 128), F32),
            pltpu.VMEM((1, 128), F32),
            pltpu.VMEM((1, 128), F32),
            pltpu.VMEM((1, 128), F32),
            pltpu.VMEM((512, 384), BF),
            pltpu.VMEM((128, 384), BF),
            pltpu.VMEM((128, 384), BF),
            pltpu.VMEM((1024, 384), BF),
            pltpu.VMEM((128, 1536), BF),
            pltpu.VMEM((64, 384), BF),
            pltpu.VMEM((4, 384, 512), BF),
            pltpu.VMEM((4, ND * 8, 128), F32),
            pltpu.VMEM((4, ND, 8, 128), F32),
            pltpu.VMEM((16, 4, 32, 128), F32),
            pltpu.VMEM((4, 128, 512), F32),
            pltpu.VMEM((4, 128, 512), F32),
            pltpu.VMEM((512, 512), BF),
            pltpu.VMEM((512, 512), BF),
            pltpu.VMEM((256, 512), BF),
            pltpu.VMEM((256, 512), BF),
            pltpu.VMEM((2, ND * 8, 128), F32),
            pltpu.VMEM((2, ND * 8, 128), F32),
            pltpu.VMEM((4, 256, 128), F32),
            pltpu.SemaphoreType.DMA((PHASES,)),
            pltpu.SemaphoreType.DMA((PHASES,)),
            pltpu.SemaphoreType.REGULAR((NZ,)),
            pltpu.SemaphoreType.DMA((12,)),
        ],
        compiler_params=pltpu.CompilerParams(
            collective_id=0, has_side_effects=True, vmem_limit_bytes=56 * 1024 * 1024
        ),
        name="triangle",
    )(
        pair.reshape(2, 4, 8, 32, 128),
        gain_in.reshape(1, 128),
        w_in,
        w_gate,
        w_out,
        gain_prod.reshape(1, 128),
        gain_trans.reshape(1, 128),
        w_ti,
        w_to,
        w_dist.T,
    )
    result = pl.pallas_call(
        add_mirrored,
        grid=(2,),
        out_shape=jax.ShapeDtypeStruct((64, 32, 64), F32),
        in_specs=[
            pl.BlockSpec((4, 8, 1, 16, 128), lambda a: (0, 0, a, 0, 0)),
            pl.BlockSpec((4, 8, 16, 128), lambda a: (0, 0, a, 0)),
            pl.BlockSpec((1, 64), lambda a: (0, 0)),
        ],
        out_specs=pl.BlockSpec((32, 32, 64), lambda a: (a, 0, 0)),
        name="add_mirrored",
    )(own, mirrored, bias.reshape(1, 64))
    return result.reshape(1, 64, 32, 64)


def solution(mesh):
    return jax.shard_map(
        shards,
        mesh=mesh,
        in_specs=(P("crop", "row", "col", None), P(), P(), P(), P(), P(), P(), P(), P(), P(), P()),
        out_specs=P("crop", "row", "col", None),
        check_vma=False,
    )
```
